32 devices in a mesh: groups: 2 (over x), ctx: 16 (over z, y, core).
Axes of the slice: x: 2, y: 2, z: 4, core: 2. Of those that a mesh axis runs over, the one named last changes fastest.
Arguments:
- raster_tokens: bfloat16 [4096, 1024], P(('groups', 'ctx')), parts along dimension 0, may hold values from -45 to 45
- hilbert_perm: int32 [4096], P(('groups', 'ctx')), parts along dimension 0, may hold values from 0 to 2047, as said below
- neighbors: int32 [32, 5], P(('groups', 'ctx')), parts along dimension 0, may hold values from 0 to 15, as said below
- neighbor_counts: int32 [32], P(('groups', 'ctx')), parts along dimension 0, may hold values from 1 to 5, as said below
- norm_gain: float32 [1024], replicated, may hold values from 0.1 to 1.9
- w_qkv: bfloat16 [1024, 3072], replicated, may hold values from -0.8125 to 0.8125
- w_out: bfloat16 [1024, 1024], replicated, may hold values from -0.5 to 0.5
- cotangent: bfloat16 [4096, 1024], P(('groups', 'ctx')), parts along dimension 0, may hold values from -6 to 6
Outputs:
- layer_out: bfloat16 [4096, 1024], P(('groups', 'ctx')), parts along dimension 0
- grad_tokens: bfloat16 [4096, 1024], P(('groups', 'ctx')), parts along dimension 0
- grad_w_out: float32 [2048, 1024], P(('groups', 'ctx')), parts along dimension 0
- grad_gain: float32 [2048], P('groups'), parts along dimension 0
The draws below stay inside these ranges and needn't reach their ends.
There are 2 independent parts, one for each index of `groups`. The reference program is written for one: setup_inputs(seed, part) draws one part's arguments, and reference() takes and returns one part's arrays. A program takes and returns all parts, laid end to end along the dimension named above; an argument that names none is the same for every part. Nothing has to cross between parts.
Inputs may be any that keep to these rules, and one draw needn't show every extreme that they name: `hilbert_perm`: A permutation. Every 128 consecutive positions of the Hilbert order take exactly 8 tokens from every 128 consecutive raster tokens. `neighbors`: row b starts with b, followed by distinct blocks other than b at a distance of at most 4; entries from slot neighbor_counts[b] on equal b. `neighbor_counts`: the block itself is counted.
All inputs are finite; a program needn't handle non-finite values.
Results may differ from the reference program's by a relative error of at most 0.02.
The reference program's roundings to bfloat16 on the way count: a program that leaves them out, or rounds other values in their place, can miss the bound.
Values may be sent and summed in bfloat16 or wider, within the bound.
A program may use at most 128 MiB of HBM per device.

```python
import math
import jax
import jax.numpy as jnp
from jax import lax

D = 1024
HEADS = 16
HD = 64
BLOCK = 128
MOST = 5
REACH = 4
TOK_DEV = 128
TOKENS = 2048
BPD = 1
NBLK = 16
WIN_DEV = 4
N_CTX = 16


def perm_core(key):
    dev_count = TOKENS // TOK_DEV
    per_peer = TOK_DEV // dev_count
    key_slots, key_rows = jax.random.split(jax.random.fold_in(key, 11))
    slot_perm = jax.vmap(lambda sub_key: jax.random.permutation(sub_key, TOK_DEV))(jax.random.split(key_slots, dev_count))
    row_perm = jax.vmap(lambda sub_key: jax.random.permutation(sub_key, TOK_DEV))(jax.random.split(key_rows, dev_count))
    source_dev = slot_perm // per_peer
    rank_in = slot_perm % per_peer
    dest_dev = jnp.arange(dev_count)[:, None]
    picked = row_perm[source_dev, dest_dev * per_peer + rank_in]
    return (source_dev * TOK_DEV + picked).reshape(-1).astype(jnp.int32)


def adjacency_core(key):
    key_pick, key_count, key_force = jax.random.split(jax.random.fold_in(key, 7), 3)
    offsets = jnp.concatenate([jnp.arange(-REACH, 0), jnp.arange(1, REACH + 1)])
    blocks = jnp.arange(NBLK)[:, None]
    candidate = blocks + offsets[None, :]
    inside = (candidate >= 0) & (candidate < NBLK)
    ranking = jax.random.randint(key_pick, (NBLK, 2 * REACH), 0, 4096) * (2 * REACH) + jnp.arange(2 * REACH)[None, :]
    ranking = jnp.where(inside, ranking, -1)
    top_values, top_index = lax.top_k(ranking, MOST - 1)
    chosen = jnp.take_along_axis(candidate, top_index, axis=1)
    counts = jax.random.randint(key_count, (NBLK,), 1, MOST + 1)
    forced = jax.random.randint(key_force, (), 0, NBLK)
    counts = jnp.where(jnp.arange(NBLK) == forced, MOST, counts)
    slot_ids = jnp.arange(1, MOST)[None, :]
    chosen = jnp.where(slot_ids < counts[:, None], chosen, blocks)
    lists = jnp.concatenate([blocks, chosen], axis=1).astype(jnp.int32)
    return (lists, counts.astype(jnp.int32))


def draw_hilbert_perm(key, part):
    return perm_core(key)


def draw_neighbors(key, part):
    lists, counts = adjacency_core(key)
    return lists


def draw_neighbor_counts(key, part):
    lists, counts = adjacency_core(key)
    return counts


def draw_raster_tokens(key, part):
    key_base, key_rows, key_cols = jax.random.split(jax.random.fold_in(key, 3), 3)
    normal_part = jax.random.truncated_normal(key_base, -4.0, 4.0, (TOKENS, D), jnp.float32)
    row_scale = jnp.exp(jax.random.uniform(key_rows, (TOKENS, 1), jnp.float32, math.log(0.3), math.log(3.0)))
    col_scale = jnp.exp(jax.random.uniform(key_cols, (1, D), jnp.float32, math.log(0.3), math.log(3.0)))
    values = normal_part * row_scale * col_scale
    return values.astype(jnp.bfloat16)


def draw_w_qkv(key, part):
    key_base = jax.random.fold_in(jax.random.fold_in(key, 5), 0)
    normal_part = jax.random.truncated_normal(key_base, -4.0, 4.0, (D, 3 * D), jnp.float32) * D ** (-0.5)
    return normal_part.astype(jnp.bfloat16)


def level_of(key, extent, cuts, low, top_value):
    def one(axis_at, shards_of):
        steps = jax.random.uniform(jax.random.fold_in(jax.random.fold_in(key, 6), axis_at), (shards_of,), jnp.float32, low / len(cuts), top_value / len(cuts))
        return jnp.repeat(jnp.exp(steps), extent[axis_at] // shards_of).reshape((-1,) + (1,) * (len(extent) - axis_at - 1))

    gain = one(*cuts[0])
    for cut in cuts[1:]:
        gain = gain * one(*cut)
    return gain


def normal_values(stream_key, shape, width, limit, shards=(), held_as=jnp.bfloat16):
    values = jax.random.normal(stream_key, shape, jnp.float32) * width
    if len(shards) > 0:
        values = level_of(stream_key, shape, shards, -0.22, 0.18) * values
    return jnp.clip(values, min=-limit, max=limit).astype(held_as)


def setup_inputs(seed: int = 0, part: int = 0) -> dict:
    key_list = jax.random.split(jax.random.key(seed), 9)
    own_keys = jax.random.split(jax.random.fold_in(key_list[8], part), 9)
    return {
        "raster_tokens": draw_raster_tokens(jax.random.fold_in(jax.random.fold_in(key_list[8], part), 71), part),
        "hilbert_perm": draw_hilbert_perm(jax.random.fold_in(jax.random.fold_in(key_list[8], part), 71), part),
        "neighbors": draw_neighbors(jax.random.fold_in(jax.random.fold_in(key_list[8], part), 71), part),
        "neighbor_counts": draw_neighbor_counts(jax.random.fold_in(jax.random.fold_in(key_list[8], part), 71), part),
        "norm_gain": jnp.clip(1.0 + 0.18 * jax.random.normal(key_list[4], (D,), jnp.float32), 0.1, 1.9),
        "w_qkv": draw_w_qkv(jax.random.fold_in(key_list[8], 71), part),
        "w_out": normal_values(key_list[6], (D, D), (D // 8) ** -0.5, 0.5),
        "cotangent": normal_values(own_keys[7], (TOKENS, D), 1.0, 6.0, ((0, 16),)),
    }


EPS = 1e-06
FAR = -1e+30

def probs_of(heads_q, heads_k, counts):
    scores = jnp.einsum('sqhd,skhd->shqk', heads_q.astype(jnp.float32), heads_k.astype(jnp.float32), precision=lax.Precision.HIGHEST) * HD ** (-0.5)
    slot_of = jnp.arange(heads_k.shape[1]) // BLOCK
    usable = slot_of[None, :] < counts[:, None]
    scores = jnp.where(usable[:, None, None, :], scores, FAR)
    row_max = lax.optimization_barrier(jnp.max(scores, axis=-1, keepdims=True))
    shifted = jnp.exp(scores - row_max)
    return shifted / lax.optimization_barrier(jnp.sum(shifted, axis=-1, keepdims=True))

def reference(raster_tokens, hilbert_perm, neighbors, neighbor_counts, norm_gain, w_qkv, w_out, cotangent):
    ordered = raster_tokens[hilbert_perm]
    ordered_f = ordered.astype(jnp.float32)
    inv_rms = lax.rsqrt(lax.optimization_barrier(jnp.mean(ordered_f * ordered_f, axis=-1, keepdims=True)) + EPS)
    normed = (ordered_f * inv_rms * norm_gain).astype(jnp.bfloat16)
    projected = jnp.dot(normed, w_qkv, preferred_element_type=jnp.float32).astype(jnp.bfloat16)
    queries = projected[:, :D]
    keys_vals = projected[:, D:]
    pad_rows = WIN_DEV * TOK_DEV
    span_rows = (2 * WIN_DEV + 1) * TOK_DEV
    kv_pad = jnp.pad(keys_vals, ((pad_rows, pad_rows), (0, 0)))
    dev_ids = jnp.arange(N_CTX, dtype=jnp.int32)

    def local_view(dev_index):
        window = lax.dynamic_slice_in_dim(kv_pad, dev_index * TOK_DEV, span_rows, 0)
        blocks = window.reshape(-1, BLOCK, 2 * D)
        lists = lax.dynamic_slice_in_dim(neighbors, dev_index * BPD, BPD, 0)
        slot_index = (lists - (dev_index - WIN_DEV) * BPD).astype(jnp.int32)
        picked = blocks[slot_index].reshape(BPD, MOST * BLOCK, 2 * D)
        heads_k = picked[:, :, :D].reshape(BPD, MOST * BLOCK, HEADS, HD)
        heads_v = picked[:, :, D:].reshape(BPD, MOST * BLOCK, HEADS, HD)
        q_rows = lax.dynamic_slice_in_dim(queries, dev_index * TOK_DEV, TOK_DEV, 0)
        heads_q = q_rows.reshape(BPD, BLOCK, HEADS, HD)
        counts = lax.dynamic_slice_in_dim(neighbor_counts, dev_index * BPD, BPD, 0)
        weights_f = probs_of(heads_q, heads_k, counts)
        return (heads_q, heads_k, heads_v, slot_index, weights_f)

    def forward_pass(dev_index):
        heads_q, heads_k, heads_v, slot_index, weights_f = local_view(dev_index)
        probs_b = weights_f.astype(jnp.bfloat16)
        out_rows = jnp.einsum('shqk,skhd->sqhd', probs_b.astype(jnp.float32), heads_v.astype(jnp.float32), precision=lax.Precision.HIGHEST)
        return out_rows.reshape(TOK_DEV, D).astype(jnp.bfloat16)
    attended = lax.map(forward_pass, dev_ids).reshape(TOKENS, D)
    projected_out = jnp.dot(attended, w_out, preferred_element_type=jnp.float32)
    layer_out = (ordered_f + projected_out).astype(jnp.bfloat16)
    norm_scale = TOKENS ** (-0.5)
    grad_w_out = lax.dot_general(attended, cotangent, (((0,), (0,)), ((), ())), preferred_element_type=jnp.float32) * norm_scale
    d_attended = jnp.dot(cotangent, w_out.T, preferred_element_type=jnp.float32).astype(jnp.bfloat16)

    def backward_pass(dev_index):
        heads_q, heads_k, heads_v, slot_index, weights_f = local_view(dev_index)
        probs_b = weights_f.astype(jnp.bfloat16)
        d_rows = lax.dynamic_slice_in_dim(d_attended, dev_index * TOK_DEV, TOK_DEV, 0)
        d_heads = d_rows.reshape(BPD, BLOCK, HEADS, HD).astype(jnp.float32)
        d_probs = jnp.einsum('sqhd,skhd->shqk', d_heads, heads_v.astype(jnp.float32), precision=lax.Precision.HIGHEST)
        row_dots = lax.optimization_barrier(jnp.sum(d_probs * weights_f, axis=-1, keepdims=True))
        d_scores = (weights_f * (d_probs - row_dots) * HD ** (-0.5)).astype(jnp.bfloat16).astype(jnp.float32)
        d_query = jnp.einsum('shqk,skhd->sqhd', d_scores, heads_k.astype(jnp.float32), precision=lax.Precision.HIGHEST)
        d_query = d_query.reshape(TOK_DEV, D).astype(jnp.bfloat16)
        d_keys = jnp.einsum('shqk,sqhd->skhd', d_scores, heads_q.astype(jnp.float32), precision=lax.Precision.HIGHEST)
        d_vals = jnp.einsum('shqk,sqhd->skhd', probs_b.astype(jnp.float32), d_heads, precision=lax.Precision.HIGHEST)
        contrib = jnp.concatenate([d_keys.reshape(BPD * MOST, BLOCK, D), d_vals.reshape(BPD * MOST, BLOCK, D)], axis=-1)
        summed = jnp.zeros(((2 * WIN_DEV + 1) * BPD, BLOCK, 2 * D), jnp.float32).at[slot_index.reshape(-1)].add(contrib)
        return (d_query, summed.reshape(span_rows, 2 * D).astype(jnp.bfloat16))
    d_query_all, partials = lax.map(backward_pass, dev_ids)
    d_query_all = d_query_all.reshape(TOKENS, D)
    partials = partials.reshape(N_CTX, 2 * WIN_DEV + 1, TOK_DEV, 2 * D)
    accum = jnp.zeros((N_CTX, TOK_DEV, 2 * D), jnp.float32)
    for offset in range(2 * WIN_DEV + 1):
        layer_piece = partials[:, offset].astype(jnp.float32)
        padded = jnp.pad(layer_piece, ((WIN_DEV, WIN_DEV), (0, 0), (0, 0)))
        accum = accum + padded[2 * WIN_DEV - offset:2 * WIN_DEV - offset + N_CTX]
    d_kv = accum.reshape(TOKENS, 2 * D).astype(jnp.bfloat16)
    d_proj = jnp.concatenate([d_query_all, d_kv], axis=-1)
    d_normed = jnp.dot(d_proj, w_qkv.T, preferred_element_type=jnp.float32)
    grad_gain = lax.optimization_barrier(jnp.sum(d_normed * ordered_f * inv_rms, axis=0)) * norm_scale
    scaled = d_normed * norm_gain
    d_ordered = cotangent.astype(jnp.float32) + inv_rms * scaled - ordered_f * inv_rms ** 3 * lax.optimization_barrier(jnp.mean(scaled * ordered_f, axis=-1, keepdims=True))
    d_ordered = d_ordered.astype(jnp.bfloat16)
    grad_tokens = jnp.zeros_like(raster_tokens).at[hilbert_perm].set(d_ordered)
    return (layer_out, grad_tokens, grad_w_out, grad_gain)
```

```python
import functools

import jax
import jax.numpy as jnp
from jax import lax
from jax.experimental import pallas as pl
from jax.experimental.pallas import tpu as pltpu
from jax.sharding import PartitionSpec as P

HEADS = 16
BLOCK = 128
REACH = 4
MOST = 5
EPS = 1e-06
FAR = -1e30
PLANE = 4
ROWS = 16
TILE = 256
F32 = jnp.float32
BF16 = jnp.bfloat16
MESH = pl.DeviceIdType.MESH


def dot(a, b):
    return jnp.dot(a, b, preferred_element_type=F32)


def dot_t(a, b):
    return lax.dot_general(a, b, (((1,), (1,)), ((), ())), preferred_element_type=F32)


def kernel(
    n,
    perm_ref, nb_ref, cnt_ref, raster_ref, gain_ref, wqkv_hbm, wout_hbm, cot_ref,
    layer_ref, gtok_ref, gwout_ref, ggain_ref,
    wqkv, wout, e_ref, s_ref, req_out, req_in, tok_out, tok_in, ret_out, ret_in,
    gain_all, ordered, q_ref, da_ref, att_ref, dq_ref, win, sel, kv, dkvt, contrib, self_t,
    pair_out, pair_in, sum_out, sum_in, at_out, at_all, cot_all, gw_out, gw_in, dord,
    a2a, wsend, wrecv, psend, precv, bsend, brecv, psem, gsend, grecv, wsem,
):
    tok, width = raster_ref.shape
    per_peer = tok // n
    folds = ROWS // per_peer
    chunk = width // folds
    rows = n * ROWS
    hd = width // HEADS
    scale = hd ** (-0.5)
    norm_scale = (tok * n) ** (-0.5)
    planes = n // PLANE
    own_rows = width // n
    me = lax.axis_index("ctx")
    partner = me + 1 - 2 * lax.rem(me, 2)
    odd = lax.rem(me, 2)
    plane = me // PLANE
    spot = lax.rem(me, PLANE)

    def remote(src, dst, ssem, rsem, dev):
        return pltpu.make_async_remote_copy(
            src_ref=src, dst_ref=dst, send_sem=ssem, recv_sem=rsem,
            device_id={"ctx": dev}, device_id_type=MESH,
        )

    w1 = pltpu.make_async_copy(wqkv_hbm, wqkv, wsem.at[0])
    w2 = pltpu.make_async_copy(wout_hbm, wout, wsem.at[1])
    w1.start()
    w2.start()
    barrier = pltpu.get_barrier_semaphore()

    @pl.loop(1, n)
    def _(k):
        pl.semaphore_signal(
            barrier, inc=1, device_id={"ctx": lax.rem(me + k, n)}, device_id_type=MESH
        )

    shift = tok.bit_length() - 1
    perm = perm_ref[...]
    src = perm >> shift
    local = (perm & (tok - 1)).astype(F32)
    ii = lax.broadcasted_iota(jnp.int32, (tok, tok), 0)
    jj = lax.broadcasted_iota(jnp.int32, (tok, tok), 1)
    src_f = jnp.broadcast_to(src.astype(F32), (tok, tok))
    src_col = jnp.sum(jnp.where(ii == jj, src_f, 0.0), axis=1, keepdims=True)
    rank = jnp.sum(jnp.where((src_col == src_f) & (ii < jj), 1.0, 0.0), axis=0, keepdims=True)
    rank = rank.astype(jnp.int32)
    kk = lax.broadcasted_iota(jnp.int32, (rows, tok), 0)
    hit = ((kk >> (ROWS.bit_length() - 1)) == src) & ((kk & (per_peer - 1)) == rank)
    e_ref[...] = jnp.where(hit, 1.0, 0.0)
    want = jnp.sum(jnp.where(hit, local, 0.0), axis=1, keepdims=True).astype(jnp.int32)
    req_out[...] = jnp.broadcast_to(want, (rows, tok)).reshape(n, ROWS, tok)
    req_in[me] = req_out[me]

    pl.semaphore_wait(barrier, n - 1)

    def a2a_copy(kind, k, src, dst, landed, mine):
        peer = lax.rem(me + k, n)
        source = lax.rem(me + n - k, n)
        return remote(
            src.at[me if mine else peer], dst.at[source if landed else me],
            a2a.at[kind, 0, k], a2a.at[kind, 1, k], peer,
        )

    def a2a_start(kind, src, dst, mine=False):
        @pl.loop(1, n)
        def _(k):
            a2a_copy(kind, k, src, dst, False, mine).start()

    def a2a_recv(kind, src, dst, mine=False):
        @pl.loop(1, n)
        def _(k):
            a2a_copy(kind, k, src, dst, True, mine).wait_recv()

    def a2a_sent(kind, src, dst, mine=False):
        @pl.loop(1, n)
        def _(k):
            a2a_copy(kind, k, src, dst, True, mine).wait_send()

    fold_shift = per_peer.bit_length() - 1

    def pack(onehot, x_ref, out):
        total = None
        fold = (kk >> fold_shift) & (folds - 1)
        for f in range(folds):
            part = dot(
                jnp.where(fold == f, onehot, 0.0).astype(BF16),
                x_ref[:, f * chunk : (f + 1) * chunk],
            )
            total = part if total is None else total + part
        out[...] = total.astype(BF16).reshape(n, ROWS, chunk)

    def unpack(onehot, y_ref, out):
        turned = onehot.T
        kt = lax.broadcasted_iota(jnp.int32, (tok, rows), 1)
        fold = (kt >> fold_shift) & (folds - 1)
        y = y_ref[...].reshape(rows, chunk)
        for f in range(folds):
            out[:, f * chunk : (f + 1) * chunk] = dot(
                jnp.where(fold == f, turned, 0.0).astype(BF16), y
            ).astype(BF16)

    a2a_start(0, req_out, req_in)
    a2a_recv(0, req_out, req_in)
    s_ref[...] = jnp.where(
        req_in[...].reshape(rows, tok) == lax.broadcasted_iota(jnp.int32, (rows, tok), 1), 1.0, 0.0
    )
    pack(s_ref[...], raster_ref, tok_out)
    a2a_start(1, tok_out, tok_in)
    tok_in[me] = tok_out[me]
    a2a_sent(0, req_out, req_in)
    a2a_recv(1, tok_out, tok_in)
    unpack(e_ref[...], tok_in, ordered)
    ord_f = ordered[...].astype(F32)
    inv_rms = lax.rsqrt(jnp.mean(ord_f * ord_f, axis=-1, keepdims=True) + EPS)
    gain = gain_ref[...]
    win[REACH] = (ord_f * inv_rms * gain).astype(BF16)

    def inside(b):
        return (b >= 0) & (b < n)

    hops = (-2, 2, -4, 4)

    def win_copy(t):
        return remote(win.at[REACH], win.at[REACH - t], wsend.at[REACH - t], wrecv.at[REACH - t], me + t)

    delta = me - partner

    def pass_copy(e):
        slot = REACH + e + delta
        return remote(win.at[REACH + e], win.at[slot], wsend.at[slot], wrecv.at[slot], partner)

    for t in hops:
        @pl.when(inside(me + t))
        def _():
            win_copy(t).start()
    pass_copy(0).start()

    w1.wait()
    w2.wait()

    @pl.loop(0, width // TILE)
    def _(t):
        cols = pl.ds(pl.multiple_of(t * TILE, TILE), TILE)
        q_ref[:, cols] = (dot(win[REACH], wqkv[:, cols]).astype(BF16).astype(F32) * scale).astype(BF16)
        da_ref[:, cols] = dot_t(cot_ref[...], wout[cols, :]).astype(BF16)

    def passes(e):
        near = inside(me + e)
        if e == -4:
            return near & (odd == 1)
        if e == 4:
            return near & (odd == 0)
        return near

    def arrive(e):
        slot = REACH + e
        return remote(win.at[REACH], win.at[slot], wsend.at[slot], wrecv.at[slot], partner)

    for e in hops:
        @pl.when(inside(me + e))
        def _():
            arrive(e).wait_recv()

        @pl.when(passes(e))
        def _():
            pass_copy(e).start()

    for e in (-1, 1, -3, 3):
        @pl.when(inside(me + e))
        def _():
            arrive(e).wait_recv()

    base = plane * PLANE

    def mate(k):
        return base + lax.rem(spot + k, PLANE)

    def cot_copy(k, where):
        return remote(cot_ref, cot_all.at[where], psem.at[0, 0, k], psem.at[0, 1, k], mate(k))

    for k in range(1, PLANE):
        cot_copy(k, spot).start()
    cot_all[spot] = cot_ref[...]

    for j in range(MOST):
        sel[j * BLOCK : (j + 1) * BLOCK, :] = win[
            jnp.clip(nb_ref[0, j] - me + REACH, 0, 2 * REACH)
        ]

    @pl.loop(0, 2 * width // TILE)
    def _(t):
        cols = pl.ds(pl.multiple_of(t * TILE, TILE), TILE)
        wcols = pl.ds(pl.multiple_of(width + t * TILE, TILE), TILE)
        kv[:, cols] = dot(sel[...], wqkv[:, wcols]).astype(BF16)

    count = cnt_ref[0]
    keys = MOST * BLOCK
    slot_of = lax.broadcasted_iota(jnp.int32, (1, keys), 1) >> (BLOCK.bit_length() - 1)
    bias = jnp.where(slot_of < count, 0.0, FAR)
    pair = 2 * hd
    low = lax.broadcasted_iota(jnp.int32, (tok, pair), 1) < hd
    blocks_per_pair = pair // own_rows

    def stacked(x):
        x = x.astype(F32)
        return jnp.concatenate([jnp.where(low, x, 0.0), jnp.where(low, 0.0, x)], axis=0)

    @pl.loop(0, HEADS // 2)
    def _(h):
        cols = pl.ds(pl.multiple_of(h * pair, pair), pair)
        vcols = pl.ds(pl.multiple_of(width + h * pair, pair), pair)
        qs = stacked(q_ref[:, cols])
        ds = stacked(da_ref[:, cols])
        k = kv[:, cols]
        v = kv[:, vcols]
        scores = dot_t(qs.astype(BF16), k) + bias
        top = jnp.max(scores, axis=-1, keepdims=True)
        raised = jnp.exp(scores - top)
        probs = raised * (1.0 / jnp.sum(raised, axis=-1, keepdims=True))
        probs_b = probs.astype(BF16)
        out = dot(probs_b, v)
        att = jnp.where(low, out[:tok], out[tok:])
        att_ref[:, cols] = att.astype(BF16)
        att_t = att.T.astype(BF16)
        for b in range(blocks_per_pair):
            block = h * blocks_per_pair + b
            at_out[lax.rem(block, PLANE) * planes + block // PLANE] = att_t[
                b * own_rows : (b + 1) * own_rows
            ]
        d_probs = dot_t(ds.astype(BF16), v)
        dots = jnp.sum(d_probs * probs, axis=-1, keepdims=True)
        d_scores = (probs * (d_probs - dots)).astype(BF16)
        dq = dot(d_scores, k) * scale
        dq_ref[:, cols] = jnp.where(low, dq[:tok], dq[tok:]).astype(BF16)
        dkvt[cols, :] = dot(qs.T.astype(BF16), d_scores).astype(BF16)
        dkvt[vcols, :] = dot(ds.T.astype(BF16), probs_b).astype(BF16)

    def at_copy(k, where):
        return remote(
            at_out.at[pl.ds(lax.rem(spot + k, PLANE) * planes, planes)], at_all.at[where],
            psem.at[1, 0, k], psem.at[1, 1, k], mate(k),
        )

    for k in range(1, PLANE):
        at_copy(k, spot).start()
    at_all[spot] = at_out[pl.ds(spot * planes, planes)]

    contrib[MOST] = jnp.zeros((width, BLOCK), BF16)

    @pl.loop(0, width // TILE)
    def _(t):
        at = pl.ds(pl.multiple_of(t * TILE, TILE), TILE)
        part = dot(wqkv[at, width:], dkvt[...])
        self_t[at, :] = part[:, :BLOCK]
        part = part.astype(BF16)
        for j in range(MOST):
            contrib[j, at, :] = part[:, j * BLOCK : (j + 1) * BLOCK]

    def holder(w):
        found = jnp.int32(MOST)
        for j in range(1, MOST):
            found = jnp.where((nb_ref[0, j] - me + REACH == w) & (j < count), j, found)
        return found

    def pair_copy(m):
        return remote(pair_out.at[m], pair_in.at[m], psend.at[m], precv.at[m], partner)

    for m, d in enumerate((-3, -1, 1, 3)):
        pair_out[m] = contrib[holder(REACH + d)]
        pair_copy(m).start()

    def from_pair(e):
        m = e // 2 + 1 + odd
        got = pair_in[jnp.clip(m, 0, 3)].astype(F32)
        if e == -4:
            return jnp.where(odd == 1, got, 0.0)
        if e == 4:
            return jnp.where(odd == 0, got, 0.0)
        return got

    def sum_copy(t):
        return remote(
            sum_out.at[REACH + t], sum_in.at[REACH - t], bsend.at[REACH - t], brecv.at[REACH - t], me + t
        )

    for m in range(4):
        pair_copy(m).wait_recv()
    for t in hops:
        @pl.when(inside(me + t))
        def _():
            both = contrib[holder(REACH + t)].astype(F32) + from_pair(t)
            sum_out[REACH + t] = both.astype(BF16)
            sum_copy(t).start()

    for k in range(1, PLANE):
        here = lax.rem(spot + PLANE - k, PLANE)
        cot_copy(k, here).wait_recv()
        at_copy(k, here).wait_recv()
    lhs = jnp.concatenate([at_all[i].reshape(width // PLANE, tok) for i in range(PLANE)], axis=1)

    @pl.loop(0, width // TILE)
    def _(t):
        cols = pl.ds(pl.multiple_of(t * TILE, TILE), TILE)
        part = dot(lhs, cot_all[:, :, cols].reshape(PLANE * tok, TILE)).reshape(planes, own_rows, TILE)
        gw_out[:, :, cols] = part.astype(BF16)

    def gw_copy(k, where):
        to = lax.rem(plane + k, planes)
        return remote(
            gw_out.at[to], gw_in.at[where], gsend.at[k], grecv.at[k], to * PLANE + spot
        )

    @pl.loop(1, planes)
    def _(k):
        gw_copy(k, plane).start()

    gw_in[plane] = gw_out[plane]

    @pl.loop(0, width // TILE)
    def _(t):
        cols = pl.ds(pl.multiple_of(t * TILE, TILE), TILE)
        layer_ref[:, cols] = (
            ordered[:, cols].astype(F32) + dot(att_ref[...], wout[:, cols])
        ).astype(BF16)

    self_t[...] += from_pair(0)
    for t in hops:
        @pl.when(inside(me + t))
        def _():
            slot = REACH + t
            remote(
                sum_out.at[slot], sum_in.at[slot], bsend.at[slot], brecv.at[slot], partner
            ).wait_recv()
            self_t[...] += sum_in[slot].astype(F32)

    d_normed = self_t[...].T + dot_t(dq_ref[...], wqkv[:, :width])
    gain_all[me] = jnp.sum(d_normed * ord_f * inv_rms, axis=0, keepdims=True)
    a2a_start(3, gain_all, gain_all, True)
    scaled = d_normed * gain
    dord[...] = (
        cot_ref[...].astype(F32)
        + inv_rms * scaled
        - ord_f * (inv_rms * inv_rms * inv_rms) * jnp.mean(scaled * ord_f, axis=-1, keepdims=True)
    ).astype(BF16)
    pack(e_ref[...], dord, ret_out)
    a2a_start(2, ret_out, ret_in)
    ret_in[me] = ret_out[me]

    @pl.loop(1, planes)
    def _(k):
        gw_copy(k, lax.rem(plane + planes - k, planes)).wait_recv()

    total = gw_in[0].astype(F32)
    for z in range(1, planes):
        total = total + gw_in[z].astype(F32)
    gwout_ref[...] = total * norm_scale

    a2a_recv(3, gain_all, gain_all, True)
    ggain_ref[...] = jnp.sum(gain_all[...], axis=0) * norm_scale
    a2a_recv(2, ret_out, ret_in)
    unpack(s_ref[...], ret_in, gtok_ref)

    a2a_sent(1, tok_out, tok_in)
    a2a_sent(2, ret_out, ret_in)
    a2a_sent(3, gain_all, gain_all, True)
    for t in hops:
        @pl.when(inside(me + t))
        def _():
            win_copy(t).wait_send()
            sum_copy(t).wait_send()

        @pl.when(passes(t))
        def _():
            pass_copy(t).wait_send()
    pass_copy(0).wait_send()
    for m in range(4):
        pair_copy(m).wait_send()
    for k in range(1, PLANE):
        cot_copy(k, spot).wait_send()
        at_copy(k, spot).wait_send()

    @pl.loop(1, planes)
    def _(k):
        gw_copy(k, plane).wait_send()


def per_device(
    raster_tokens, hilbert_perm, neighbors, neighbor_counts, norm_gain, w_qkv, w_out, cotangent
):
    n = lax.axis_size("ctx")
    tok, width = raster_tokens.shape
    per_peer = tok // n
    assert tok == BLOCK and n % PLANE == 0 and ROWS % per_peer == 0
    chunk = width * per_peer // ROWS
    planes = n // PLANE
    own_rows = width // n
    rows = n * ROWS
    vmem = pl.BlockSpec(memory_space=pltpu.VMEM)
    smem = pl.BlockSpec(memory_space=pltpu.SMEM)
    hbm = pl.BlockSpec(memory_space=pl.ANY)
    V = pltpu.VMEM
    dma = pltpu.SemaphoreType.DMA
    span = 2 * REACH + 1
    scratch = [
        V((width, 3 * width), BF16),
        V((width, width), BF16),
        V((rows, tok), F32),
        V((rows, tok), F32),
        V((n, ROWS, tok), jnp.int32),
        V((n, ROWS, tok), jnp.int32),
        V((n, ROWS, chunk), BF16),
        V((n, ROWS, chunk), BF16),
        V((n, ROWS, chunk), BF16),
        V((n, ROWS, chunk), BF16),
        V((n, 1, width), F32),
        V((tok, width), BF16),
        V((tok, width), BF16),
        V((tok, width), BF16),
        V((tok, width), BF16),
        V((tok, width), BF16),
        V((span, tok, width), BF16),
        V((MOST * BLOCK, width), BF16),
        V((MOST * BLOCK, 2 * width), BF16),
        V((2 * width, MOST * BLOCK), BF16),
        V((MOST + 1, width, BLOCK), BF16),
        V((width, tok), F32),
        V((4, width, BLOCK), BF16),
        V((4, width, BLOCK), BF16),
        V((span, width, BLOCK), BF16),
        V((span, width, BLOCK), BF16),
        V((n, own_rows, tok), BF16),
        V((PLANE, planes, own_rows, tok), BF16),
        V((PLANE, tok, width), BF16),
        V((planes, own_rows, width), BF16),
        V((planes, own_rows, width), BF16),
        V((tok, width), BF16),
        dma((4, 2, n)),
        dma((span,)),
        dma((span,)),
        dma((4,)),
        dma((4,)),
        dma((span,)),
        dma((span,)),
        dma((2, 2, PLANE)),
        dma((planes,)),
        dma((planes,)),
        dma((2,)),
    ]
    layer_out, grad_tokens, grad_w_out, grad_gain = pl.pallas_call(
        functools.partial(kernel, n),
        out_shape=(
            jax.ShapeDtypeStruct((tok, width), BF16),
            jax.ShapeDtypeStruct((tok, width), BF16),
            jax.ShapeDtypeStruct((own_rows, width), F32),
            jax.ShapeDtypeStruct((1, width), F32),
        ),
        in_specs=[vmem, smem, smem, vmem, vmem, hbm, hbm, vmem],
        out_specs=(vmem, vmem, vmem, vmem),
        scratch_shapes=scratch,
        compiler_params=pltpu.CompilerParams(
            collective_id=0, has_side_effects=True, vmem_limit_bytes=56 * 1024 * 1024
        ),
    )(
        hilbert_perm.reshape(1, tok), neighbors, neighbor_counts, raster_tokens,
        norm_gain.reshape(1, width), w_qkv, w_out, cotangent,
    )
    return (layer_out, grad_tokens, grad_w_out, grad_gain.reshape(width))


def solution(mesh):
    placed = (
        P(("groups", "ctx"), None),
        P(("groups", "ctx")),
        P(("groups", "ctx"), None),
        P(("groups", "ctx")),
        P(),
        P(),
        P(),
        P(("groups", "ctx"), None),
    )
    return jax.shard_map(
        per_device,
        mesh=mesh,
        in_specs=placed,
        out_specs=(
            P(("groups", "ctx"), None),
            P(("groups", "ctx"), None),
            P(("groups", "ctx"), None),
            P("groups"),
        ),
        check_vma=False,
    )
```
